32 devices in a mesh: edp: 8 (over y, x, core), etp: 4 (over z).
Axes of the slice: x: 2, y: 2, z: 4, core: 2. Of those that a mesh axis runs over, the one named last changes fastest.
Arguments:
- tokens: bfloat16 [4096, 3072], P('edp'), may hold values from -6 to 6
- expert_ids: int32 [4096, 2], P('edp'), may hold values from 0 to 7, as said below
- route_weight: float32 [4096, 2], P('edp'), may hold values from 0.2 to 1
- index_list: int32 [8, 256], P('edp'), may hold values from 0 to 512, as said below
- gate_weight: bfloat16 [3072, 8192], P('edp', 'etp'), may hold values from -0.109375 to 0.109375
- up_weight: bfloat16 [3072, 8192], P('edp', 'etp'), may hold values from -0.109375 to 0.109375
- down_weight: bfloat16 [8192, 3072], P('etp', 'edp'), may hold values from -0.0625 to 0.0625
Outputs:
- expert_out: bfloat16 [4096, 3072], P(('edp', 'etp'))
The draws below stay inside these ranges and needn't reach their ends.
Inputs may be any that keep to these rules, and one draw needn't show every extreme that they name: `index_list`: row b lists, increasing, the positions within block b of the tokens that name expert 0, then 512 in the remaining slots; in every draw some block is full. `expert_ids`: each token names two different experts; a token names expert 0 exactly when its position stands in its block's row of index_list.
All inputs are finite; a program needn't handle non-finite values.
Results may differ from the reference program's by a relative error of at most 0.018.
Values may be sent and summed in bfloat16 or wider, within the bound.
A program may use at most 128 MiB of HBM per device.

```python
import jax
import jax.numpy as jnp
from jax import lax

D = 3072
FF = 8192
NUM_EXPERTS = 8
TOK_DEV = 512
CAP = 256
BLOCKS = 8
TOKENS = 4096
N_ETP = 4


def routing(key):
    base_key = jax.random.fold_in(key, 7)
    k_shift, k_pick, k_perm, k_first, k_offset, k_order = jax.random.split(base_key, 6)
    halvings = jax.random.randint(k_shift, (BLOCKS,), 0, 4)
    counts = jnp.maximum(CAP // jnp.left_shift(jnp.ones_like(halvings), halvings), 1)
    full_block = jax.random.randint(k_pick, (), 0, BLOCKS)
    counts = jnp.where(jnp.arange(BLOCKS) == full_block, CAP, counts)
    perm_keys = jax.random.split(k_perm, BLOCKS)

    def permute(one_key):
        return jax.random.permutation(one_key, TOK_DEV)
    orders = jax.vmap(permute)(perm_keys)
    ranking = jnp.argsort(orders, axis=1)
    chosen = ranking < counts[:, None]
    position = jnp.arange(TOK_DEV)[None, :]
    scores = jnp.where(chosen, position, TOK_DEV + position)
    ordered = jnp.sort(scores, axis=1)[:, :CAP]
    index_list = jnp.where(ordered < TOK_DEV, ordered, TOK_DEV).astype(jnp.int32)
    first_pick = jax.random.randint(k_first, (BLOCKS, TOK_DEV), 1, NUM_EXPERTS)
    offsets = jax.random.randint(k_offset, (BLOCKS, TOK_DEV), 1, NUM_EXPERTS - 1)
    second_pick = 1 + (first_pick - 1 + offsets) % (NUM_EXPERTS - 1)
    leading = jnp.where(chosen, 0, first_pick)
    trailing = jnp.where(chosen, first_pick, second_pick)
    order_bit = jax.random.randint(k_order, (BLOCKS, TOK_DEV), 0, 2)
    left_ids = jnp.where(order_bit == 0, leading, trailing)
    right_ids = jnp.where(order_bit == 0, trailing, leading)
    expert_ids = jnp.stack([left_ids, right_ids], axis=-1).reshape(BLOCKS * TOK_DEV, 2).astype(jnp.int32)
    return (expert_ids, index_list)


def draw_expert_ids(key, part):
    return routing(key)[0]


def draw_index_list(key, part):
    return routing(key)[1]


def block_scale(rng, shape, cuts, smallest, top_value):
    factor_of = 1.0
    for dim, blocks in cuts:
        draws = jax.random.uniform(jax.random.fold_in(jax.random.fold_in(rng, 6), dim), (blocks,), jnp.float32, smallest / len(cuts), top_value / len(cuts))
        factor_of = factor_of * jnp.repeat(jnp.exp(draws), shape[dim] // blocks).reshape((-1,) + (1,) * (len(shape) - 1 - dim))
    return factor_of


def noise(rng, extent, scale, limit, shards=(), held_as=jnp.bfloat16):
    entries = jax.random.normal(rng, extent, jnp.float32) * scale
    if len(shards) > 0:
        entries = block_scale(rng, extent, shards, -0.22, 0.18) * entries
    return jnp.clip(entries, min=-limit, max=limit).astype(held_as)


def setup_inputs(seed: int = 0) -> dict:
    key_list = jax.random.split(jax.random.key(seed), 8)
    tokens = noise(key_list[0], (TOKENS, D), 1.0, 6.0, ((0, 8),))
    expert_ids = draw_expert_ids(jax.random.fold_in(key_list[7], 71), 0)
    route_weight = jnp.clip(0.2 + 0.8 * jax.random.uniform(key_list[2], (TOKENS, 2), jnp.float32) ** block_scale(key_list[2], (TOKENS, 2), ((0, 8),), -0.2, 0.2), 0.2, 1.0)
    index_list = draw_index_list(jax.random.fold_in(key_list[7], 71), 0)
    gate_weight = noise(key_list[4], (D, FF), D ** -0.5, 0.109375, ((0, 8), (1, 4)))
    up_weight = noise(key_list[5], (D, FF), D ** -0.5, 0.109375, ((0, 8), (1, 4)))
    down_weight = noise(key_list[6], (FF, D), FF ** -0.5, 0.0625, ((0, 4), (1, 8)))
    return dict(tokens=tokens, expert_ids=expert_ids, route_weight=route_weight, index_list=index_list, gate_weight=gate_weight, up_weight=up_weight, down_weight=down_weight)


def reference(tokens, expert_ids, route_weight, index_list, gate_weight, up_weight, down_weight):
    block_count = index_list.shape[0]
    block_rows = tokens.shape[0] // block_count
    combine = jnp.sum(jnp.where(expert_ids == 0, route_weight, jnp.zeros_like(route_weight)), axis=1)
    width = FF // N_ETP
    down_parts = down_weight.reshape(N_ETP, width, D).astype(jnp.float32)

    def one_block(block_index):
        row_start = (block_index * block_rows).astype(jnp.int32)
        local_rows = lax.dynamic_slice_in_dim(tokens, row_start, block_rows, 0)
        local_combine = lax.dynamic_slice_in_dim(combine, row_start, block_rows, 0)
        slot_rows = index_list[block_index].astype(jnp.int32)
        is_live = slot_rows < block_rows
        safe_rows = jnp.minimum(slot_rows, block_rows - 1).astype(jnp.int32)
        picked = jnp.take(local_rows, safe_rows, axis=0)
        row_scale = jnp.where(is_live, jnp.take(local_combine, safe_rows), jnp.zeros_like(local_combine[:1]))
        gate_sum = jnp.dot(picked, gate_weight, preferred_element_type=jnp.float32)
        up_sum = jnp.dot(picked, up_weight, preferred_element_type=jnp.float32)
        hidden = (jax.nn.silu(gate_sum) * up_sum * row_scale[:, None]).astype(jnp.bfloat16)
        pieces = hidden.reshape(CAP, N_ETP, width).astype(jnp.float32)
        partial_terms = jnp.einsum("rkf,kfd->krd", pieces, down_parts)
        rounded = lax.optimization_barrier(partial_terms.astype(jnp.bfloat16))
        shares = jnp.sum(rounded.astype(jnp.float32), axis=0).astype(jnp.bfloat16)
        empty = jnp.zeros((block_rows, D), jnp.bfloat16)
        return empty.at[slot_rows].set(shares, mode="drop")

    result = lax.map(one_block, jnp.arange(block_count, dtype=jnp.int32))
    return result.reshape(block_count * block_rows, D)
```

```python
import functools

import jax
import jax.numpy as jnp
from jax import lax
from jax.experimental import pallas as pl
from jax.experimental.pallas import tpu as pltpu
from jax.sharding import PartitionSpec as P

MESH = pl.DeviceIdType.MESH
BF16 = jnp.bfloat16
F32 = jnp.float32


def dot(a, b):
    return jnp.dot(a, b, preferred_element_type=F32)


def kernel(
    n, ranks, parts,
    gate_hbm, up_hbm, down_hbm, tok_hbm, idx_row, idx_col, comb,
    out_ref,
    tok, x_own, x_other, x_send, w_gate, w_up, down, part_send, part_recv, part_own, hidden, placing, z_send, z_recv,
    tok_sem, x_sems, w_recv, w_sib, w_far, p_send, p_recv, d_recv, d_sib, d_far, d_fwd, s_send, s_recv,
):
    e = lax.axis_index("edp")
    t = lax.axis_index("etp")
    group = n // 2
    chips = group // 2
    h, g = e // group, e % group
    q, c = g // 2, g % 2
    rows, width = gate_hbm.shape
    cols = down_hbm.shape[1]
    slots = idx_col.shape[0]
    depth = group * rows
    piece = width // parts

    def at(hh, qq, cc):
        return hh * group + qq * 2 + cc

    sibling = (at(h, q, 1 - c), t)
    partner = (at(1 - h, q, c), t)

    def far(k):
        return (q + k) % chips

    def remote(src, dst, send, recv, dev):
        return pltpu.make_async_remote_copy(
            src_ref=src, dst_ref=dst, send_sem=send, recv_sem=recv, device_id=dev, device_id_type=MESH
        )

    barrier = pltpu.get_barrier_semaphore()
    pl.semaphore_signal(barrier, inc=1, device_id=sibling, device_id_type=MESH)

    @pl.loop(1, 2 * chips)
    def _(m):
        dev = (at((h + m // chips) % 2, (q + m % chips) % chips, c), t)
        pl.semaphore_signal(barrier, inc=1, device_id=dev, device_id_type=MESH)

    @pl.loop(1, ranks)
    def _(k):
        pl.semaphore_signal(barrier, inc=1, device_id=(e, (t + k) % ranks), device_id_type=MESH)

    tok_copy = pltpu.make_async_copy(tok_hbm, tok, tok_sem)
    tok_copy.start()
    pl.semaphore_wait(barrier, 2 * chips + ranks - 1)

    weights = ((gate_hbm, w_gate), (up_hbm, w_up))

    def w_src(i, f):
        return weights[i][0].at[:, pl.ds(f * piece, piece)]

    def w_dst(i, f, gg):
        return weights[i][1].at[pl.ds(pl.multiple_of(gg * rows, 32), rows), pl.ds(f * piece, piece)]

    def w_far_copy(i, f, k):
        return remote(w_src(i, f), w_dst(i, f, g), w_far.at[f, i, k - 1], w_recv.at[f, i, g], (at(h, far(k), c), t))

    def w_local(i, f):
        return pltpu.make_async_copy(w_src(i, f), w_dst(i, f, g), w_recv.at[f, i, g])

    def w_own_sib(i, f):
        return remote(w_src(i, f), w_dst(i, f, g), w_sib.at[f, i, 0], w_recv.at[f, i, g], sibling)

    def w_relay(i, f, k):
        gg = far(k) * 2 + c
        return remote(w_dst(i, f, gg), w_dst(i, f, gg), w_sib.at[f, i, k], w_recv.at[f, i, gg], sibling)

    def w_arrived(i, f, gg):
        ref = w_dst(i, f, gg)
        remote(ref, ref, w_sib.at[f, i, 0], w_recv.at[f, i, gg], sibling).wait_recv()

    def start_far(f):
        for i in range(2):
            for k in range(1, chips):
                w_far_copy(i, f, k).start()

    def start_near(f):
        for i in range(2):
            w_local(i, f).start()
            w_own_sib(i, f).start()

    start_far(0)
    start_near(0)
    if parts > 1:
        start_far(1)

    tok_copy.wait()
    tokens_in = tok.shape[0]
    hit = lax.broadcasted_iota(jnp.int32, (slots, tokens_in), 1) == idx_col[...]
    scale = jnp.sum(jnp.where(hit, comb[...], 0.0), axis=1, keepdims=True)
    pick = hit.astype(F32).astype(BF16)
    mine = pl.ds(pl.multiple_of(h * depth, 128), depth)
    theirs = pl.ds(pl.multiple_of((1 - h) * depth, 128), depth)
    x_send[...] = dot(pick, tok[:, theirs]).astype(BF16)
    x_copy = remote(x_send, x_other, x_sems.at[0], x_sems.at[1], partner)
    x_copy.start()
    x_own[...] = dot(pick, tok[:, mine]).astype(BF16)
    placing[...] = (
        lax.broadcasted_iota(jnp.int32, (tokens_in, slots), 0) == idx_row[...]
    ).astype(F32).astype(BF16)
    for f in range(1, parts):
        start_near(f)

    def part_copy(i, f):
        span = pl.ds(f * piece, piece)
        return remote(part_send.at[i, :, span], part_recv.at[i, :, span], p_send.at[f, i], p_recv.at[f, i], partner)

    def gather(f):
        for i in range(2):
            for k in range(1, chips):
                w_arrived(i, f, far(k) * 2 + c)
                w_relay(i, f, k).start()
        if f + 2 < parts:
            for i in range(2):
                for k in range(1, chips):
                    w_far_copy(i, f, k).wait_send()
            start_far(f + 2)
        if f == 0:
            x_copy.wait_recv()
        for i in range(2):
            w_local(i, f).wait()
            w_arrived(i, f, q * 2 + 1 - c)
            for k in range(1, chips):
                w_arrived(i, f, far(k) * 2 + 1 - c)
            wref = weights[i][1]
            tile = min(piece, 256)

            @pl.loop(0, piece // tile)
            def _(m):
                span = pl.ds(pl.multiple_of(f * piece + m * tile, 128), tile)
                part_send[i, :, span] = dot(x_other[...], wref[:, span]).astype(BF16)

            part_copy(i, f).start()

            @pl.loop(0, piece // tile)
            def _(m):
                span = pl.ds(pl.multiple_of(f * piece + m * tile, 128), tile)
                part_own[i, :, span] = dot(x_own[...], wref[:, span])

    def activate(f):
        for i in range(2):
            part_copy(i, f).wait_recv()
        span = pl.ds(f * piece, piece)
        gate = part_own[0, :, span] + part_recv[0, :, span].astype(F32)
        up = part_own[1, :, span] + part_recv[1, :, span].astype(F32)
        hidden[:, span] = (gate / (1.0 + jnp.exp(-gate)) * up * scale).astype(BF16)

    def d_own(dev, sem):
        return remote(down_hbm, down.at[e], sem, d_recv.at[e], dev)

    def d_far_copy(k):
        return d_own((at(h, far(k), c), t), d_far.at[k])

    def d_local():
        return pltpu.make_async_copy(down_hbm, down.at[e], d_recv.at[e])

    def d_relay(m, s):
        return remote(down.at[s], down.at[s], d_sib.at[m], d_recv.at[s], sibling)

    def d_arrived(s):
        remote(down.at[s], down.at[s], d_sib.at[0], d_recv.at[s], sibling).wait_recv()

    def forward(k):
        s = jnp.where(c == 0, at(h, far(k), c), at(1 - h, q, c))
        dev = jnp.where(c == 0, at(1 - h, q, c), at(h, far(k), c))
        return remote(down.at[s], down.at[s], d_fwd.at[k - 1], d_recv.at[s], (dev, t))

    def start_down():
        for k in range(1, chips):
            d_far_copy(k).start()
        d_local().start()
        d_own(sibling, d_sib.at[0]).start()

    for f in range(parts):
        gather(f)
        if f == parts - 1:
            start_down()
            d_own(partner, d_far.at[0]).start()
        if f >= 1:
            activate(f - 1)
    activate(parts - 1)

    def z_copy(s, k):
        peer = (t + k) % ranks
        return remote(z_send.at[s, peer], z_recv.at[s, t], s_send.at[s, peer], s_recv.at[s, t], (e, peer))

    def share(s):
        part = dot(hidden[...], down[s]).astype(BF16)
        placed = dot(placing[...], part).astype(BF16)
        z_send[s] = placed.reshape(ranks, tokens_in // ranks, cols)

        @pl.loop(1, ranks)
        def _(k):
            z_copy(s, k).start()

    d_local().wait()
    share(e)
    near = at(h, q, 1 - c)
    d_arrived(near)
    share(near)

    @pl.loop(1, 2 * chips)
    def _(m):
        hh, qq = (h + m // chips) % 2, (q + m % chips) % chips
        s = at(hh, qq, c)
        d_arrived(s)

        @pl.when(jnp.logical_and(c == 0, m < chips))
        def _():
            remote(down.at[s], down.at[s], d_fwd.at[m - 1], d_recv.at[s], partner).start()

        @pl.when(jnp.logical_and(c == 1, m == chips))
        def _():
            for k in range(1, chips):
                remote(down.at[s], down.at[s], d_fwd.at[k - 1], d_recv.at[s], (at(h, far(k), c), t)).start()

        d_relay(m, s).start()
        share(s)
        other = at(hh, qq, 1 - c)
        d_arrived(other)
        share(other)

    @pl.loop(0, n)
    def _(s):
        total = z_send[s, t].astype(F32)
        for k in range(1, ranks):
            src = (t + k) % ranks
            remote(z_send.at[s, src], z_recv.at[s, src], s_send.at[s, src], s_recv.at[s, src], (e, src)).wait_recv()
            total = total + z_recv[s, src].astype(F32)
        out_ref[s] = total.astype(BF16)

    x_copy.wait_send()
    for f in range(parts):
        for i in range(2):
            w_own_sib(i, f).wait_send()
            part_copy(i, f).wait_send()
            for k in range(1, chips):
                w_relay(i, f, k).wait_send()
                if f + 2 >= parts:
                    w_far_copy(i, f, k).wait_send()
    d_own(sibling, d_sib.at[0]).wait_send()
    d_own(partner, d_far.at[0]).wait_send()
    for k in range(1, chips):
        d_far_copy(k).wait_send()
        forward(k).wait_send()

    @pl.loop(1, 2 * chips)
    def _(m):
        d_relay(m, at((h + m // chips) % 2, (q + m % chips) % chips, c)).wait_send()

    @pl.loop(0, n)
    def _(s):
        @pl.loop(1, ranks)
        def _(k):
            z_copy(s, k).wait_send()


def shards(n, ranks, tokens, expert_ids, route_weight, index_list, gate_weight, up_weight, down_weight):
    tokens_in, model = tokens.shape
    slots = index_list.shape[1]
    rows, width = gate_weight.shape
    cols = down_weight.shape[1]
    group = n // 2
    chips = group // 2
    depth = group * rows
    parts = 4
    combine = jnp.sum(jnp.where(expert_ids == 0, route_weight, jnp.zeros_like(route_weight)), axis=1)
    share = tokens_in // ranks
    hbm = pl.BlockSpec(memory_space=pl.ANY)
    vmem = pl.BlockSpec(memory_space=pltpu.VMEM)
    dma = pltpu.SemaphoreType.DMA
    out = pl.pallas_call(
        functools.partial(kernel, n, ranks, parts),
        out_shape=jax.ShapeDtypeStruct((n, share, cols), BF16),
        in_specs=[hbm, hbm, hbm, hbm, vmem, vmem, vmem],
        out_specs=vmem,
        scratch_shapes=[
            pltpu.VMEM((tokens_in, model), BF16),
            pltpu.VMEM((slots, depth), BF16),
            pltpu.VMEM((slots, depth), BF16),
            pltpu.VMEM((slots, depth), BF16),
            pltpu.VMEM((depth, width), BF16),
            pltpu.VMEM((depth, width), BF16),
            pltpu.VMEM((n, width, cols), BF16),
            pltpu.VMEM((2, slots, width), BF16),
            pltpu.VMEM((2, slots, width), BF16),
            pltpu.VMEM((2, slots, width), F32),
            pltpu.VMEM((slots, width), BF16),
            pltpu.VMEM((tokens_in, slots), BF16),
            pltpu.VMEM((n, ranks, share, cols), BF16),
            pltpu.VMEM((n, ranks, share, cols), BF16),
            dma,
            dma((2,)),
            dma((parts, 2, group)),
            dma((parts, 2, chips)),
            dma((parts, 2, chips)),
            dma((parts, 2)),
            dma((parts, 2)),
            dma((n,)),
            dma((2 * chips,)),
            dma((chips,)),
            dma((chips,)),
            dma((n, ranks)),
            dma((n, ranks)),
        ],
        compiler_params=pltpu.CompilerParams(
            collective_id=0, has_side_effects=True, vmem_limit_bytes=60 * 1024 * 1024
        ),
        cost_estimate=pl.CostEstimate(
            flops=2 * slots * model * width * 3, bytes_accessed=3 * n * rows * width * 2, transcendentals=slots * width
        ),
    )(
        gate_weight, up_weight, down_weight, tokens,
        index_list, index_list.reshape(slots, 1), combine.reshape(1, tokens_in),
    )
    return out.transpose(1, 0, 2).reshape(share, model)


def solution(mesh):
    in_specs = (
        P("edp", None),
        P("edp", None),
        P("edp", None),
        P("edp", None),
        P("edp", "etp"),
        P("edp", "etp"),
        P("etp", "edp"),
    )
    out_specs = P(("edp", "etp"), None)
    body = functools.partial(shards, mesh.shape["edp"], mesh.shape["etp"])
    return jax.shard_map(body, mesh=mesh, in_specs=in_specs, out_specs=out_specs, check_vma=False)
```

```python
import functools

import jax
import jax.numpy as jnp
from jax import lax
from jax.experimental import pallas as pl
from jax.experimental.pallas import tpu as pltpu
from jax.sharding import PartitionSpec as P

MESH = pl.DeviceIdType.MESH
BF16 = jnp.bfloat16
F32 = jnp.float32


def dot(a, b):
    return jnp.dot(a, b, preferred_element_type=F32)


def kernel(
    n, ranks, parts,
    gate_hbm, up_hbm, down_hbm, tok_hbm, idx_row, idx_col, comb,
    out_ref,
    tok, x_own, x_other, x_send, w_gate, w_up, down, part_send, part_recv, part_own, hidden, placing, z_send, z_recv,
    tok_sem, x_sems, w_recv, w_sib, w_far, p_send, p_recv, d_recv, d_sib, d_far, d_fwd, s_send, s_recv,
):
    e = lax.axis_index("edp")
    t = lax.axis_index("etp")
    group = n // 2
    chips = group // 2
    h, g = e // group, e % group
    q, c = g // 2, g % 2
    rows, width = gate_hbm.shape
    cols = down_hbm.shape[1]
    slots = idx_col.shape[0]
    depth = group * rows
    piece = width // parts

    def at(hh, qq, cc):
        return hh * group + qq * 2 + cc

    sibling = (at(h, q, 1 - c), t)
    partner = (at(1 - h, q, c), t)

    def far(k):
        return (q + k) % chips

    def remote(src, dst, send, recv, dev):
        return pltpu.make_async_remote_copy(
            src_ref=src, dst_ref=dst, send_sem=send, recv_sem=recv, device_id=dev, device_id_type=MESH
        )

    barrier = pltpu.get_barrier_semaphore()
    pl.semaphore_signal(barrier, inc=1, device_id=sibling, device_id_type=MESH)

    @pl.loop(1, 2 * chips)
    def _(m):
        dev = (at((h + m // chips) % 2, (q + m % chips) % chips, c), t)
        pl.semaphore_signal(barrier, inc=1, device_id=dev, device_id_type=MESH)

    @pl.loop(1, ranks)
    def _(k):
        pl.semaphore_signal(barrier, inc=1, device_id=(e, (t + k) % ranks), device_id_type=MESH)

    tok_copy = pltpu.make_async_copy(tok_hbm, tok, tok_sem)
    tok_copy.start()
    pl.semaphore_wait(barrier, 2 * chips + ranks - 1)

    weights = ((gate_hbm, w_gate), (up_hbm, w_up))

    def w_src(i, f):
        return weights[i][0].at[:, pl.ds(f * piece, piece)]

    def w_dst(i, f, gg):
        return weights[i][1].at[pl.ds(pl.multiple_of(gg * rows, 32), rows), pl.ds(f * piece, piece)]

    def w_far_copy(i, f, k):
        return remote(w_src(i, f), w_dst(i, f, g), w_far.at[f, i, k - 1], w_recv.at[f, i, g], (at(h, far(k), c), t))

    def w_local(i, f):
        return pltpu.make_async_copy(w_src(i, f), w_dst(i, f, g), w_recv.at[f, i, g])

    def w_own_sib(i, f):
        return remote(w_src(i, f), w_dst(i, f, g), w_sib.at[f, i, 0], w_recv.at[f, i, g], sibling)

    def w_relay(i, f, k):
        gg = far(k) * 2 + c
        return remote(w_dst(i, f, gg), w_dst(i, f, gg), w_sib.at[f, i, k], w_recv.at[f, i, gg], sibling)

    def w_arrived(i, f, gg):
        ref = w_dst(i, f, gg)
        remote(ref, ref, w_sib.at[f, i, 0], w_recv.at[f, i, gg], sibling).wait_recv()

    def start_far(f):
        for i in range(2):
            for k in range(1, chips):
                w_far_copy(i, f, k).start()

    def start_near(f):
        for i in range(2):
            w_local(i, f).start()
            w_own_sib(i, f).start()

    start_far(0)
    start_near(0)
    if parts > 1:
        start_far(1)

    tok_copy.wait()
    tokens_in = tok.shape[0]
    hit = lax.broadcasted_iota(jnp.int32, (slots, tokens_in), 1) == idx_col[...]
    scale = jnp.sum(jnp.where(hit, comb[...], 0.0), axis=1, keepdims=True)
    pick = hit.astype(F32).astype(BF16)
    mine = pl.ds(pl.multiple_of(h * depth, 128), depth)
    theirs = pl.ds(pl.multiple_of((1 - h) * depth, 128), depth)
    x_send[...] = dot(pick, tok[:, theirs]).astype(BF16)
    x_copy = remote(x_send, x_other, x_sems.at[0], x_sems.at[1], partner)
    x_copy.start()
    x_own[...] = dot(pick, tok[:, mine]).astype(BF16)
    placing[...] = (
        lax.broadcasted_iota(jnp.int32, (tokens_in, slots), 0) == idx_row[...]
    ).astype(F32).astype(BF16)
    for f in range(1, parts):
        start_near(f)

    def part_copy(i, f):
        span = pl.ds(f * piece, piece)
        return remote(part_send.at[i, :, span], part_recv.at[i, :, span], p_send.at[f, i], p_recv.at[f, i], partner)

    def gather(f):
        for i in range(2):
            for k in range(1, chips):
                w_arrived(i, f, far(k) * 2 + c)
                w_relay(i, f, k).start()
        if f == parts - 1:
            start_down()
        if f + 2 < parts:
            for i in range(2):
                for k in range(1, chips):
                    w_far_copy(i, f, k).wait_send()
            start_far(f + 2)
        if f == 0:
            x_copy.wait_recv()
        for i in range(2):
            w_local(i, f).wait()
            w_arrived(i, f, q * 2 + 1 - c)
            for k in range(1, chips):
                w_arrived(i, f, far(k) * 2 + 1 - c)
            wref = weights[i][1]
            tile = min(piece, 256)

            @pl.loop(0, piece // tile)
            def _(m):
                span = pl.ds(pl.multiple_of(f * piece + m * tile, 128), tile)
                part_send[i, :, span] = dot(x_other[...], wref[:, span]).astype(BF16)

            part_copy(i, f).start()

            @pl.loop(0, piece // tile)
            def _(m):
                span = pl.ds(pl.multiple_of(f * piece + m * tile, 128), tile)
                part_own[i, :, span] = dot(x_own[...], wref[:, span])

    def activate(f):
        for i in range(2):
            part_copy(i, f).wait_recv()
        span = pl.ds(f * piece, piece)
        gate = part_own[0, :, span] + part_recv[0, :, span].astype(F32)
        up = part_own[1, :, span] + part_recv[1, :, span].astype(F32)
        hidden[:, span] = (gate / (1.0 + jnp.exp(-gate)) * up * scale).astype(BF16)

    def d_own(dev, sem):
        return remote(down_hbm, down.at[e], sem, d_recv.at[e], dev)

    def d_far_copy(k):
        return d_own((at(h, far(k), c), t), d_far.at[k])

    def d_local():
        return pltpu.make_async_copy(down_hbm, down.at[e], d_recv.at[e])

    def d_relay(m, s):
        return remote(down.at[s], down.at[s], d_sib.at[m], d_recv.at[s], sibling)

    def d_arrived(s):
        remote(down.at[s], down.at[s], d_sib.at[0], d_recv.at[s], sibling).wait_recv()

    def forward(k):
        s = jnp.where(c == 0, at(h, far(k), c), at(1 - h, q, c))
        dev = jnp.where(c == 0, at(1 - h, q, c), at(h, far(k), c))
        return remote(down.at[s], down.at[s], d_fwd.at[k - 1], d_recv.at[s], (dev, t))

    def start_down():
        for k in range(1, chips):
            d_far_copy(k).start()
        d_local().start()
        d_own(sibling, d_sib.at[0]).start()

    for f in range(parts):
        gather(f)
        if f == parts - 1:
            d_own(partner, d_far.at[0]).start()
        if f >= 1:
            activate(f - 1)
    activate(parts - 1)

    def z_copy(s, k):
        peer = (t + k) % ranks
        return remote(z_send.at[s, peer], z_recv.at[s, t], s_send.at[s, peer], s_recv.at[s, t], (e, peer))

    def share(s):
        part = dot(hidden[...], down[s]).astype(BF16)
        placed = dot(placing[...], part).astype(BF16)
        z_send[s] = placed.reshape(ranks, tokens_in // ranks, cols)

        @pl.loop(1, ranks)
        def _(k):
            z_copy(s, k).start()

    d_local().wait()
    share(e)
    near = at(h, q, 1 - c)
    d_arrived(near)
    share(near)

    @pl.loop(1, 2 * chips)
    def _(m):
        hh, qq = (h + m // chips) % 2, (q + m % chips) % chips
        s = at(hh, qq, c)
        d_arrived(s)

        @pl.when(jnp.logical_and(c == 0, m < chips))
        def _():
            remote(down.at[s], down.at[s], d_fwd.at[m - 1], d_recv.at[s], partner).start()

        @pl.when(jnp.logical_and(c == 1, m == chips))
        def _():
            for k in range(1, chips):
                remote(down.at[s], down.at[s], d_fwd.at[k - 1], d_recv.at[s], (at(h, far(k), c), t)).start()

        d_relay(m, s).start()
        share(s)
        other = at(hh, qq, 1 - c)
        d_arrived(other)
        share(other)

    @pl.loop(0, n)
    def _(s):
        total = z_send[s, t].astype(F32)
        for k in range(1, ranks):
            src = (t + k) % ranks
            remote(z_send.at[s, src], z_recv.at[s, src], s_send.at[s, src], s_recv.at[s, src], (e, src)).wait_recv()
            total = total + z_recv[s, src].astype(F32)
        out_ref[s] = total.astype(BF16)

    x_copy.wait_send()
    for f in range(parts):
        for i in range(2):
            w_own_sib(i, f).wait_send()
            part_copy(i, f).wait_send()
            for k in range(1, chips):
                w_relay(i, f, k).wait_send()
                if f + 2 >= parts:
                    w_far_copy(i, f, k).wait_send()
    d_own(sibling, d_sib.at[0]).wait_send()
    d_own(partner, d_far.at[0]).wait_send()
    for k in range(1, chips):
        d_far_copy(k).wait_send()
        forward(k).wait_send()

    @pl.loop(1, 2 * chips)
    def _(m):
        d_relay(m, at((h + m // chips) % 2, (q + m % chips) % chips, c)).wait_send()

    @pl.loop(0, n)
    def _(s):
        @pl.loop(1, ranks)
        def _(k):
            z_copy(s, k).wait_send()


def shards(n, ranks, tokens, expert_ids, route_weight, index_list, gate_weight, up_weight, down_weight):
    tokens_in, model = tokens.shape
    slots = index_list.shape[1]
    rows, width = gate_weight.shape
    cols = down_weight.shape[1]
    group = n // 2
    chips = group // 2
    depth = group * rows
    parts = max(1, width // 256)
    combine = jnp.sum(jnp.where(expert_ids == 0, route_weight, jnp.zeros_like(route_weight)), axis=1)
    share = tokens_in // ranks
    hbm = pl.BlockSpec(memory_space=pl.ANY)
    vmem = pl.BlockSpec(memory_space=pltpu.VMEM)
    dma = pltpu.SemaphoreType.DMA
    out = pl.pallas_call(
        functools.partial(kernel, n, ranks, parts),
        out_shape=jax.ShapeDtypeStruct((n, share, cols), BF16),
        in_specs=[hbm, hbm, hbm, hbm, vmem, vmem, vmem],
        out_specs=vmem,
        scratch_shapes=[
            pltpu.VMEM((tokens_in, model), BF16),
            pltpu.VMEM((slots, depth), BF16),
            pltpu.VMEM((slots, depth), BF16),
            pltpu.VMEM((slots, depth), BF16),
            pltpu.VMEM((depth, width), BF16),
            pltpu.VMEM((depth, width), BF16),
            pltpu.VMEM((n, width, cols), BF16),
            pltpu.VMEM((2, slots, width), BF16),
            pltpu.VMEM((2, slots, width), BF16),
            pltpu.VMEM((2, slots, width), F32),
            pltpu.VMEM((slots, width), BF16),
            pltpu.VMEM((tokens_in, slots), BF16),
            pltpu.VMEM((n, ranks, share, cols), BF16),
            pltpu.VMEM((n, ranks, share, cols), BF16),
            dma,
            dma((2,)),
            dma((parts, 2, group)),
            dma((parts, 2, chips)),
            dma((parts, 2, chips)),
            dma((parts, 2)),
            dma((parts, 2)),
            dma((n,)),
            dma((2 * chips,)),
            dma((chips,)),
            dma((chips,)),
            dma((n, ranks)),
            dma((n, ranks)),
        ],
        compiler_params=pltpu.CompilerParams(
            collective_id=0, has_side_effects=True, vmem_limit_bytes=60 * 1024 * 1024
        ),
        cost_estimate=pl.CostEstimate(
            flops=2 * slots * model * width * 3, bytes_accessed=3 * n * rows * width * 2, transcendentals=slots * width
        ),
    )(
        gate_weight, up_weight, down_weight, tokens,
        index_list, index_list.reshape(slots, 1), combine.reshape(1, tokens_in),
    )
    return out.transpose(1, 0, 2).reshape(share, model)


def solution(mesh):
    in_specs = (
        P("edp", None),
        P("edp", None),
        P("edp", None),
        P("edp", None),
        P("edp", "etp"),
        P("edp", "etp"),
        P("etp", "edp"),
    )
    out_specs = P(("edp", "etp"), None)
    body = functools.partial(shards, mesh.shape["edp"], mesh.shape["etp"])
    return jax.shard_map(body, mesh=mesh, in_specs=in_specs, out_specs=out_specs, check_vma=False)
```
